32 devices in a mesh: shot: 2 (over y), freq: 4 (over z), tile: 4 (over x, core).
Axes of the slice: x: 2, y: 2, z: 4, core: 2. Of those that a mesh axis runs over, the one named last changes fastest.
Arguments:
- omega: float32 [8], P('freq'), may hold values from 30 to 150
- wavefields: float32 [4, 2, 8, 1024, 256], P('shot', None, 'freq', 'tile'), parts along dimension 0, may hold values from -2.5 to 2.5
- velocity: float32 [2, 1024, 256], P(None, ('tile', 'freq')), may hold values from 1.5 to 4.5
- eta: float32 [2, 1024, 256], P(None, ('tile', 'freq')), may hold values from 0 to 0.3
Outputs:
- image: float32 [4, 1024, 256], P('shot', ('tile', 'freq')), parts along dimension 0
The draws below stay inside these ranges and needn't reach their ends.
There are 2 independent parts, one for each index of `shot`. The reference program is written for one: setup_inputs(seed, part) draws one part's arguments, and reference() takes and returns one part's arrays. A program takes and returns all parts, laid end to end along the dimension named above; an argument that names none is the same for every part. Nothing has to cross between parts.
All inputs are finite; a program needn't handle non-finite values.
Results may differ from the reference program's by a relative error of at most 0.0001.
Values sent between devices are 32-bit elements; how exact they have to be, the bound alone decides.
A program may use at most 64 MiB of HBM per device.

```python
import math
import jax
import jax.numpy as jnp
from jax import lax

DEPTH = 2
NY = 256
NF = 8
NX = 1024


def levels(own_key, shape, cuts, smallest, top_value):
    gain = 1.0
    for position, blocks in cuts:
        heights = jax.random.uniform(jax.random.fold_in(jax.random.fold_in(own_key, 6), position), (blocks,), jnp.float32, smallest / len(cuts), top_value / len(cuts))
        gain = gain * jnp.repeat(jnp.exp(heights), shape[position] // blocks).reshape((-1,) + (1,) * (len(shape) - 1 - position))
    return gain


def centred(rng, dims, width, limit, shards=(), kind=jnp.bfloat16):
    factor_of = levels(rng, dims, shards, -0.22, 0.18) if shards else 1.0
    result = jax.random.normal(rng, dims, jnp.float32) * width * factor_of
    return jnp.minimum(jnp.maximum(result, -limit), limit).astype(kind)


def setup_inputs(seed: int = 0, part: int = 0) -> dict:
    seeds = jax.random.split(jax.random.key(seed), 5)
    part_splits = jax.random.split(jax.random.fold_in(seeds[4], part), 5)
    return {
        "omega": jnp.clip(jnp.exp(math.log(150.0) - 1.609438 * jax.random.uniform(seeds[0], (NF,), jnp.float32) ** levels(seeds[0], (NF,), ((0, 4),), -0.2, 0.2)), 30.0, 150.0),
        "wavefields": centred(part_splits[1], (2, 2, NF, NX, NY), 0.35, 2.5, ((2, 4), (3, 4)), jnp.float32),
        "velocity": jnp.clip(1.5 + 3.0 * jax.random.uniform(seeds[2], (DEPTH, NX, NY), jnp.float32) ** levels(seeds[2], (DEPTH, NX, NY), ((1, 16),), -0.2, 0.2), 1.5, 4.5),
        "eta": jnp.clip(0.3 * jax.random.uniform(seeds[3], (DEPTH, NX, NY), jnp.float32) ** levels(seeds[3], (DEPTH, NX, NY), ((1, 16),), -0.2, 0.2), 0.0, 0.3),
    }


coeffs = ((1, 1.5), (2, -0.15), (3, 1.0 / 90.0))
centre = -49.0 / 9.0
lateral_scale = 0.5
depth_step = 0.01


def stencil(padded):
    rows = padded.shape[-2] - 6
    cols = padded.shape[-1] - 6
    core = padded[..., 3:3 + rows, 3:3 + cols]
    total = 2.0 * centre * core
    for shift, weight in coeffs:
        part = padded[..., 3 + shift:3 + shift + rows, 3:3 + cols] + padded[..., 3 - shift:3 - shift + rows, 3:3 + cols]
        part = part + padded[..., 3:3 + rows, 3 + shift:3 + shift + cols] + padded[..., 3:3 + rows, 3 - shift:3 - shift + cols]
        total = total + weight * part
    return total


def advance(field, lap, vel, eta_d, om):
    signs = jnp.array([-1.0, 1.0], jnp.float32).reshape((2,) + (1,) * (field.ndim - 2))
    real_part, imag_part = field[:, 0], field[:, 1]
    lap_re, lap_im = lap[:, 0], lap[:, 1]
    theta = lateral_scale * vel * (1.0 + 2.0 * eta_d) / om
    v_re = real_part - signs * theta * lap_im
    v_im = imag_part + signs * theta * lap_re
    phase = om * depth_step / vel
    cosine = jnp.cos(phase)
    sine = signs * jnp.sin(phase)
    out_re = cosine * v_re - sine * v_im
    out_im = cosine * v_im + sine * v_re
    term = out_re[0] * out_re[1] + out_im[0] * out_im[1]
    return jnp.stack([out_re, out_im], axis=1), term


def reference(omega, wavefields, velocity, eta):
    fields = jnp.moveaxis(wavefields, 2, 0)
    images = []
    for depth in range(DEPTH):
        vel = velocity[depth]
        eta_d = eta[depth]

        def one(item):
            field, om = item
            padded = jnp.pad(field, ((0, 0), (0, 0), (3, 3), (3, 3)))
            lap = stencil(padded)
            return advance(field, lap, vel, eta_d, om)

        fields, terms = lax.map(one, (fields, omega))
        images.append(jnp.sum(terms, axis=0))
    return jnp.stack(images)
```

```python
import functools

import jax
import jax.numpy as jnp
from jax import lax
from jax.experimental import pallas as pl
from jax.experimental.pallas import tpu as pltpu
from jax.sharding import PartitionSpec as P

MESH = pl.DeviceIdType.MESH
PAD = 16
HALO = 8

CENTRE = -980.0
WEIGHTS = ((1, 135.0), (2, -13.5), (3, 1.0))


def band(distance, centre):
    out = jnp.where(distance == 0, centre, 0.0)
    for shift, weight in WEIGHTS:
        out = jnp.where(jnp.abs(distance) == shift, weight, out)
    return out.astype(jnp.bfloat16)


def cos_sin(x):
    z = x * x
    c = -1.0 / 3628800.0
    for k in (1.0 / 40320.0, -1.0 / 720.0, 1.0 / 24.0, -0.5, 1.0):
        c = c * z + k
    s = 1.0 / 362880.0
    for k in (-1.0 / 5040.0, 1.0 / 120.0, -1.0 / 6.0, 1.0):
        s = s * z + k
    return c, s * x


def kernel(n, tiles, omega_ref, wf, vel, eta, out, a_buf, b_buf, va, term, rbuf,
           my_buf, mx_buf, local_sem, zs, zr, ys, yr, hs, hr, rs, rr):
    depths = vel.shape[0]
    shard = vel.shape[1]
    rows, cols = wf.shape[3], wf.shape[4]
    freqs = wf.shape[2]
    me = lax.axis_index("freq")
    shot = lax.axis_index("shot")
    tile = lax.axis_index("tile")
    other = 1 - shot
    has_up = tile > 0
    has_down = tile < tiles - 1

    def rows_of(o):
        return pl.ds(pl.multiple_of(o * shard, shard), shard)

    load_v = pltpu.make_async_copy(vel, va.at[0, :, rows_of(me)], local_sem.at[0])
    load_e = pltpu.make_async_copy(eta, va.at[1, :, rows_of(me)], local_sem.at[1])
    load_f = pltpu.make_async_copy(wf, a_buf.at[:, :, :, pl.ds(PAD, rows)], local_sem.at[2])
    load_v.start()
    load_e.start()
    load_f.start()

    barrier = pltpu.get_barrier_semaphore()

    def greet(k, carry):
        @pl.when(k != me)
        def _():
            pl.semaphore_signal(barrier, inc=1, device_id={"freq": k}, device_id_type=MESH)
        return carry

    lax.fori_loop(0, n, greet, 0)
    pl.semaphore_signal(barrier, inc=1, device_id={"shot": other}, device_id_type=MESH)

    @pl.when(has_up)
    def _():
        pl.semaphore_signal(barrier, inc=1, device_id={"tile": tile - 1}, device_id_type=MESH)

    @pl.when(has_down)
    def _():
        pl.semaphore_signal(barrier, inc=1, device_id={"tile": tile + 1}, device_id_type=MESH)

    r = lax.broadcasted_iota(jnp.int32, (cols, cols), 0)
    c = lax.broadcasted_iota(jnp.int32, (cols, cols), 1)
    my = band(r - c, CENTRE)
    my_buf[0:cols] = my
    my_buf[cols:2 * cols] = my
    window = shard + 2 * PAD
    r = lax.broadcasted_iota(jnp.int32, (shard, window), 0)
    c = lax.broadcasted_iota(jnp.int32, (shard, window), 1)
    mx_buf[:, 0:window] = band(c - PAD - r, 0.0)
    for buf in (a_buf, b_buf):
        zeros = jnp.zeros(buf.shape[:3] + (PAD - HALO, cols), jnp.float32)
        buf[:, :, :, 0:PAD - HALO] = zeros
        buf[:, :, :, PAD + rows + HALO:2 * PAD + rows] = zeros

        @pl.when(jnp.logical_not(has_up))
        def _():
            buf[:, :, :, PAD - HALO:PAD] = jnp.zeros(buf.shape[:3] + (HALO, cols), jnp.float32)

        @pl.when(jnp.logical_not(has_down))
        def _():
            buf[:, :, :, PAD + rows:PAD + rows + HALO] = jnp.zeros(buf.shape[:3] + (HALO, cols), jnp.float32)

    pl.semaphore_wait(barrier, n + has_up.astype(jnp.int32) + has_down.astype(jnp.int32))

    def halo(d, slot):
        if d == 0:
            src = wf.at[:, :, :, pl.ds(0 if slot == 0 else rows - HALO, HALO)]
            buf = a_buf
        else:
            src = b_buf.at[:, :, :, pl.ds(PAD if slot == 0 else PAD + rows - HALO, HALO)]
            buf = b_buf
        dst = buf.at[:, :, :, pl.ds(PAD + rows if slot == 0 else PAD - HALO, HALO)]
        return pltpu.make_async_remote_copy(
            src_ref=src, dst_ref=dst, send_sem=hs.at[d, slot], recv_sem=hr.at[d, slot],
            device_id={"tile": tile - 1 if slot == 0 else tile + 1}, device_id_type=MESH)

    def on_line(d, o, way):
        slot = va.at[shot, d, rows_of(o)]
        return pltpu.make_async_remote_copy(
            src_ref=slot, dst_ref=slot, send_sem=zs.at[way, d, o], recv_sem=zr.at[d, o],
            device_id={"freq": me + 1 if way else me - 1}, device_id_type=MESH)

    def across(d, o, which):
        slot = va.at[which, d, rows_of(o)]
        return pltpu.make_async_remote_copy(
            src_ref=slot, dst_ref=slot, send_sem=ys.at[d, o], recv_sem=yr.at[d, o],
            device_id={"shot": other}, device_id_type=MESH)

    def summand(d, to, frm):
        return pltpu.make_async_remote_copy(
            src_ref=term.at[d, rows_of(to)], dst_ref=rbuf.at[d, rows_of(frm)],
            send_sem=rs.at[d, to], recv_sem=rr.at[d, frm],
            device_id={"freq": to}, device_id_type=MESH)

    def send_own(d):
        @pl.when(me < n - 1)
        def _():
            on_line(d, me, 1).start()

        @pl.when(me > 0)
        def _():
            on_line(d, me, 0).start()

    def pass_on(d, dist):
        low, high = me - dist, me + dist

        @pl.when(low >= 0)
        def _():
            on_line(d, low, 1).wait_recv()

            @pl.when(me < n - 1)
            def _():
                on_line(d, low, 1).start()
            across(d, low, shot).start()

        @pl.when(high < n)
        def _():
            on_line(d, high, 0).wait_recv()

            @pl.when(me > 0)
            def _():
                on_line(d, high, 0).start()
            across(d, high, shot).start()

    mesh_rows = (shard, cols)

    def block(d, o, src, dst):
        start = pl.multiple_of(o * shard, shard)
        v = va[0, d, pl.ds(start, shard)]
        e = va[1, d, pl.ds(start, shard)]
        inv = 1.0 / v
        lift = v * (1.0 + 2.0 * e) * (0.5 / 90.0)
        mx = mx_buf[:, 0:window]
        mx2 = jnp.concatenate([mx, mx], axis=1)
        total = None
        for w in range(freqs):
            om = jnp.full((1, cols), omega_ref[w], jnp.float32)
            theta = lift * (1.0 / om)
            cosine, sine = cos_sin(inv * (om * 0.01))
            mids, along, lhs = [], [], []
            for s in range(2):
                for k in range(2):
                    f = src[s, k, w, pl.ds(start, window)]
                    hi = f.astype(jnp.bfloat16)
                    lo = (f - hi.astype(jnp.float32)).astype(jnp.bfloat16)
                    mids.append(f[PAD:PAD + shard])
                    along.append(jnp.dot(mx2, jnp.concatenate([hi, lo], axis=0),
                                         preferred_element_type=jnp.float32))
                    lhs.append(jnp.concatenate([hi[PAD:PAD + shard], lo[PAD:PAD + shard]], axis=1))
            ydir = jnp.dot(jnp.concatenate(lhs, axis=0), my_buf[...], preferred_element_type=jnp.float32)
            laps = [along[i] + ydir[i * shard:(i + 1) * shard] for i in range(4)]
            outs = []
            for s in range(2):
                sign = -1.0 if s == 0 else 1.0
                re, im = mids[2 * s], mids[2 * s + 1]
                lre, lim = theta * laps[2 * s], theta * laps[2 * s + 1]
                if s == 0:
                    vre, vim = re + lim, im - lre
                    ore = cosine * vre + sine * vim
                    oim = cosine * vim - sine * vre
                else:
                    vre, vim = re - lim, im + lre
                    ore = cosine * vre - sine * vim
                    oim = cosine * vim + sine * vre
                outs.append((ore, oim))
                if dst is not None:
                    at = pl.ds(pl.multiple_of(start + PAD, 8), shard)
                    dst[s, 0, w, at] = ore
                    dst[s, 1, w, at] = oim
            part = outs[0][0] * outs[1][0] + outs[0][1] * outs[1][1]
            total = part if total is None else total + part
        term[d, pl.ds(start, shard)] = total

        @pl.when(o != me)
        def _():
            summand(d, o, me).start()

    @pl.when(has_up)
    def _():
        halo(0, 0).start()

    @pl.when(has_down)
    def _():
        halo(0, 1).start()

    load_v.wait()
    load_e.wait()
    send_own(0)
    load_f.wait()

    def halo_wait(d, o):
        @pl.when(jnp.logical_and(o == 0, has_up))
        def _():
            halo(d, 1).wait_recv()

        @pl.when(jnp.logical_and(o == n - 1, has_down))
        def _():
            halo(d, 0).wait_recv()

    def first(s, carry):
        @pl.when(s < n)
        def _():
            pass_on(0, s)

        @pl.when(s == 1)
        def _():
            for d in range(1, depths):
                send_own(d)

        @pl.when(s > 1)
        def _():
            for d in range(1, depths):
                pass_on(d, s - 1)

        def one(way, carry):
            o = jnp.where(way == 0, me - (s - 1), me + (s - 1))

            @pl.when(jnp.logical_and(jnp.logical_and(o >= 0, o < n),
                                     jnp.logical_or(way == 0, s > 1)))
            def _():
                @pl.when(s > 1)
                def _():
                    across(0, o, other).wait_recv()
                halo_wait(0, o)
                block(0, o, a_buf, b_buf)

                @pl.when(jnp.logical_and(o == 0, has_up))
                def _():
                    halo(1, 0).start()

                @pl.when(jnp.logical_and(o == n - 1, has_down))
                def _():
                    halo(1, 1).start()
            return carry

        lax.fori_loop(0, 2, one, 0)
        return carry

    lax.fori_loop(1, n + 1, first, 0)

    def second(i, carry):
        o = jnp.where(i < n - 2, i + 1, jnp.where(i == n - 2, 0, n - 1))

        @pl.when(o != me)
        def _():
            across(1, o, other).wait_recv()
        halo_wait(1, o)
        block(1, o, b_buf, None)
        return carry

    lax.fori_loop(0, n, second, 0)

    for d in range(depths):
        total = term[d, rows_of(me)]

        def add(k, total):
            o = lax.rem(me + k, n)
            summand(d, o, o).wait_recv()
            return total + rbuf[d, rows_of(o)]

        out[d] = lax.fori_loop(1, n, add, total)

    for d in range(depths):
        @pl.when(has_up)
        def _():
            halo(d, 0).wait_send()

        @pl.when(has_down)
        def _():
            halo(d, 1).wait_send()

        def drain(o, carry):
            @pl.when(jnp.logical_and(o <= me, me < n - 1))
            def _():
                on_line(d, o, 1).wait_send()

            @pl.when(jnp.logical_and(o >= me, me > 0))
            def _():
                on_line(d, o, 0).wait_send()

            @pl.when(o != me)
            def _():
                across(d, o, shot).wait_send()
                summand(d, o, me).wait_send()
            return carry

        lax.fori_loop(0, n, drain, 0)


def per_device(n, tiles, omega, wavefields, velocity, eta):
    depths, shard, cols = velocity.shape
    sides, parts, freqs, rows, _ = wavefields.shape
    padded = (sides, parts, freqs, rows + 2 * PAD, cols)
    dma = pltpu.SemaphoreType.DMA
    return pl.pallas_call(
        functools.partial(kernel, n, tiles),
        out_shape=jax.ShapeDtypeStruct((depths, shard, cols), jnp.float32),
        in_specs=[pl.BlockSpec(memory_space=pltpu.SMEM)] + [pl.BlockSpec(memory_space=pl.ANY)] * 3,
        out_specs=pl.BlockSpec(memory_space=pltpu.VMEM),
        scratch_shapes=[
            pltpu.VMEM(padded, jnp.float32),
            pltpu.VMEM(padded, jnp.float32),
            pltpu.VMEM((2, depths, rows, cols), jnp.float32),
            pltpu.VMEM((depths, rows, cols), jnp.float32),
            pltpu.VMEM((depths, rows, cols), jnp.float32),
            pltpu.VMEM((2 * cols, cols), jnp.bfloat16),
            pltpu.VMEM((shard, shard + 2 * PAD), jnp.bfloat16),
            dma((3,)),
            dma((2, depths, n)),
            dma((depths, n)),
            dma((depths, n)),
            dma((depths, n)),
            dma((depths, 2)),
            dma((depths, 2)),
            dma((depths, n)),
            dma((depths, n)),
        ],
        compiler_params=pltpu.CompilerParams(
            collective_id=0, has_side_effects=True, vmem_limit_bytes=40 * 1024 * 1024),
    )(omega, wavefields, velocity, eta)


def solution(mesh):
    return jax.shard_map(
        functools.partial(per_device, mesh.shape["freq"], mesh.shape["tile"]),
        mesh=mesh,
        in_specs=(
            P("freq"),
            P("shot", None, "freq", "tile", None),
            P(None, ("tile", "freq"), None),
            P(None, ("tile", "freq"), None),
        ),
        out_specs=P("shot", ("tile", "freq"), None),
        check_vma=False,
    )
```

```python
import functools

import jax
import jax.numpy as jnp
from jax import lax
from jax.experimental import pallas as pl
from jax.experimental.pallas import tpu as pltpu
from jax.sharding import PartitionSpec as P

MESH = pl.DeviceIdType.MESH
CHAINED = ()
DIRECT = ()
EARLY = False
PAD = 16
HALO = 8

CENTRE = -980.0
WEIGHTS = ((1, 135.0), (2, -13.5), (3, 1.0))


def band(distance, centre):
    out = jnp.where(distance == 0, centre, 0.0)
    for shift, weight in WEIGHTS:
        out = jnp.where(jnp.abs(distance) == shift, weight, out)
    return out.astype(jnp.bfloat16)


def cos_sin(x):
    z = x * x
    c = -1.0 / 3628800.0
    for k in (1.0 / 40320.0, -1.0 / 720.0, 1.0 / 24.0, -0.5, 1.0):
        c = c * z + k
    s = 1.0 / 362880.0
    for k in (-1.0 / 5040.0, 1.0 / 120.0, -1.0 / 6.0, 1.0):
        s = s * z + k
    return c, s * x


def kernel(n, tiles, omega_hbm, wf, vel, eta, out, a_buf, b_buf, va, term, rbuf, cbuf,
           my_buf, mx_buf, omega_ref, local_sem, zs, zr, ys, yr, hs, hr, rs, rr, cr):
    depths = vel.shape[0]
    shard = vel.shape[1]
    rows, cols = wf.shape[3], wf.shape[4]
    freqs = wf.shape[2]
    me = lax.axis_index("freq")
    shot = lax.axis_index("shot")
    tile = lax.axis_index("tile")
    other = 1 - shot
    has_up = tile > 0
    has_down = tile < tiles - 1

    def rows_of(o):
        return pl.ds(pl.multiple_of(o * shard, shard), shard)

    load_v = pltpu.make_async_copy(vel, va.at[0, :, rows_of(me)], local_sem.at[0])
    load_e = pltpu.make_async_copy(eta, va.at[1, :, rows_of(me)], local_sem.at[1])
    load_f = pltpu.make_async_copy(wf, a_buf.at[:, :, :, pl.ds(PAD, rows)], local_sem.at[2])
    load_o = pltpu.make_async_copy(omega_hbm, omega_ref, local_sem.at[3])
    load_v.start()
    load_e.start()
    load_f.start()
    load_o.start()

    barrier = pltpu.get_barrier_semaphore()

    def greet(k, carry):
        @pl.when(k != me)
        def _():
            pl.semaphore_signal(barrier, inc=1, device_id={"freq": k}, device_id_type=MESH)
        return carry

    lax.fori_loop(0, n, greet, 0)
    pl.semaphore_signal(barrier, inc=1, device_id={"shot": other}, device_id_type=MESH)

    @pl.when(has_up)
    def _():
        pl.semaphore_signal(barrier, inc=1, device_id={"tile": tile - 1}, device_id_type=MESH)

    @pl.when(has_down)
    def _():
        pl.semaphore_signal(barrier, inc=1, device_id={"tile": tile + 1}, device_id_type=MESH)

    r = lax.broadcasted_iota(jnp.int32, (cols, cols), 0)
    c = lax.broadcasted_iota(jnp.int32, (cols, cols), 1)
    my = band(r - c, CENTRE)
    my_buf[0:cols] = my
    my_buf[cols:2 * cols] = my
    window = shard + 2 * PAD
    r = lax.broadcasted_iota(jnp.int32, (shard, window), 0)
    c = lax.broadcasted_iota(jnp.int32, (shard, window), 1)
    mx_buf[:, 0:window] = band(c - PAD - r, 0.0)
    for buf in (a_buf, b_buf):
        zeros = jnp.zeros(buf.shape[:3] + (PAD - HALO, cols), jnp.float32)
        buf[:, :, :, 0:PAD - HALO] = zeros
        buf[:, :, :, PAD + rows + HALO:2 * PAD + rows] = zeros

        @pl.when(jnp.logical_not(has_up))
        def _():
            buf[:, :, :, PAD - HALO:PAD] = jnp.zeros(buf.shape[:3] + (HALO, cols), jnp.float32)

        @pl.when(jnp.logical_not(has_down))
        def _():
            buf[:, :, :, PAD + rows:PAD + rows + HALO] = jnp.zeros(buf.shape[:3] + (HALO, cols), jnp.float32)

    pl.semaphore_wait(barrier, n + has_up.astype(jnp.int32) + has_down.astype(jnp.int32))

    def halo(d, slot):
        if d == 0:
            src = wf.at[:, :, :, pl.ds(0 if slot == 0 else rows - HALO, HALO)]
            buf = a_buf
        else:
            src = b_buf.at[:, :, :, pl.ds(PAD if slot == 0 else PAD + rows - HALO, HALO)]
            buf = b_buf
        dst = buf.at[:, :, :, pl.ds(PAD + rows if slot == 0 else PAD - HALO, HALO)]
        return pltpu.make_async_remote_copy(
            src_ref=src, dst_ref=dst, send_sem=hs.at[d, slot], recv_sem=hr.at[d, slot],
            device_id={"tile": tile - 1 if slot == 0 else tile + 1}, device_id_type=MESH)

    def on_line(d, o, way):
        slot = va.at[shot, d, rows_of(o)]
        return pltpu.make_async_remote_copy(
            src_ref=slot, dst_ref=slot, send_sem=zs.at[way, d, o], recv_sem=zr.at[d, o],
            device_id={"freq": me + 1 if way else me - 1}, device_id_type=MESH)

    def across(d, o, which):
        slot = va.at[which, d, rows_of(o)]
        return pltpu.make_async_remote_copy(
            src_ref=slot, dst_ref=slot, send_sem=ys.at[d, o], recv_sem=yr.at[d, o],
            device_id={"shot": other}, device_id_type=MESH)

    def summand(d, to, frm):
        return pltpu.make_async_remote_copy(
            src_ref=term.at[d, rows_of(to)], dst_ref=rbuf.at[d, rows_of(frm)],
            send_sem=rs.at[d, to], recv_sem=rr.at[d, frm],
            device_id={"freq": to}, device_id_type=MESH)

    def chain(d, o, way):
        return pltpu.make_async_remote_copy(
            src_ref=term.at[d, rows_of(o)], dst_ref=cbuf.at[way, d, rows_of(o)],
            send_sem=rs.at[d, o], recv_sem=cr.at[way, d, o],
            device_id={"freq": me + 1 if way else me - 1}, device_id_type=MESH)

    def relay(d, pos):
        def step(k, carry):
            for way, first in ((1, me == pos), (0, n - 1 - me == pos)):
                o = me + k if way else me - k

                @pl.when(jnp.logical_and(first, jnp.logical_and(o >= 0, o < n)))
                def _():
                    chain(d, o, way).wait_recv()
                    term[d, rows_of(o)] += cbuf[way, d, rows_of(o)]
                    chain(d, o, way).start()
            return carry

        lax.fori_loop(1, n, step, 0)

    def to_all(d, to):
        slot = va.at[shot, d, rows_of(me)]
        return pltpu.make_async_remote_copy(
            src_ref=slot, dst_ref=slot, send_sem=zs.at[0, d, to], recv_sem=zr.at[d, me],
            device_id={"freq": to}, device_id_type=MESH)

    def send_own(d):
        if d in DIRECT:
            def step(k, carry):
                for to in (me + k, me - k):
                    @pl.when(jnp.logical_and(to >= 0, to < n))
                    def _():
                        to_all(d, to).start()
                return carry

            lax.fori_loop(1, n, step, 0)
        else:
            @pl.when(me < n - 1)
            def _():
                on_line(d, me, 1).start()

            @pl.when(me > 0)
            def _():
                on_line(d, me, 0).start()

    def pass_on(d, dist):
        for way in (1, 0):
            o = me - dist if way else me + dist

            @pl.when(jnp.logical_and(o >= 0, o < n))
            def _():
                on_line(d, o, way).wait_recv()
                if d not in DIRECT:
                    @pl.when(me < n - 1 if way else me > 0)
                    def _():
                        on_line(d, o, way).start()
                across(d, o, shot).start()

    def block(d, o, src, dst):
        start = pl.multiple_of(o * shard, shard)
        v = va[0, d, pl.ds(start, shard)]
        e = va[1, d, pl.ds(start, shard)]
        inv = 1.0 / v
        lift = v * (1.0 + 2.0 * e) * (0.5 / 90.0)
        mx = mx_buf[:, 0:window]
        mx2 = jnp.concatenate([mx, mx], axis=1)
        total = None
        for w in range(freqs):
            om = jnp.full((1, cols), omega_ref[w], jnp.float32)
            theta = lift * (1.0 / om)
            cosine, sine = cos_sin(inv * (om * 0.01))
            mids, along, lhs = [], [], []
            for s in range(2):
                for k in range(2):
                    f = src[s, k, w, pl.ds(start, window)]
                    hi = f.astype(jnp.bfloat16)
                    lo = (f - hi.astype(jnp.float32)).astype(jnp.bfloat16)
                    mids.append(f[PAD:PAD + shard])
                    along.append(jnp.dot(mx2, jnp.concatenate([hi, lo], axis=0),
                                         preferred_element_type=jnp.float32))
                    lhs.append(jnp.concatenate([hi[PAD:PAD + shard], lo[PAD:PAD + shard]], axis=1))
            ydir = jnp.dot(jnp.concatenate(lhs, axis=0), my_buf[...], preferred_element_type=jnp.float32)
            laps = [along[i] + ydir[i * shard:(i + 1) * shard] for i in range(4)]
            outs = []
            for s in range(2):
                sign = -1.0 if s == 0 else 1.0
                re, im = mids[2 * s], mids[2 * s + 1]
                lre, lim = theta * laps[2 * s], theta * laps[2 * s + 1]
                if s == 0:
                    vre, vim = re + lim, im - lre
                    ore = cosine * vre + sine * vim
                    oim = cosine * vim - sine * vre
                else:
                    vre, vim = re - lim, im + lre
                    ore = cosine * vre - sine * vim
                    oim = cosine * vim + sine * vre
                outs.append((ore, oim))
                if dst is not None:
                    at = pl.ds(pl.multiple_of(start + PAD, 8), shard)
                    dst[s, 0, w, at] = ore
                    dst[s, 1, w, at] = oim
            part = outs[0][0] * outs[1][0] + outs[0][1] * outs[1][1]
            total = part if total is None else total + part
        term[d, pl.ds(start, shard)] = total

        if d in CHAINED:
            @pl.when(jnp.logical_and(o > me, me == 0))
            def _():
                chain(d, o, 1).start()

            @pl.when(jnp.logical_and(o < me, me == n - 1))
            def _():
                chain(d, o, 0).start()
        else:
            @pl.when(o != me)
            def _():
                summand(d, o, me).start()

    @pl.when(has_up)
    def _():
        halo(0, 0).start()

    @pl.when(has_down)
    def _():
        halo(0, 1).start()

    load_v.wait()
    load_e.wait()
    send_own(0)
    if EARLY:
        for d in range(1, depths):
            send_own(d)
    load_f.wait()
    load_o.wait()

    def halo_wait(d, o):
        @pl.when(jnp.logical_and(o == 0, has_up))
        def _():
            halo(d, 1).wait_recv()

        @pl.when(jnp.logical_and(o == n - 1, has_down))
        def _():
            halo(d, 0).wait_recv()

    def first(s, carry):
        @pl.when(s < n)
        def _():
            pass_on(0, s)

        if not EARLY:
            @pl.when(s == 1)
            def _():
                for d in range(1, depths):
                    send_own(d)

        @pl.when(jnp.logical_and(s > 1, s <= n))
        def _():
            for d in range(1, depths):
                pass_on(d, s - 1)

        def one(way, carry):
            o = jnp.where(way == 0, me - (s - 2), me + (s - 2))

            @pl.when(jnp.logical_and(jnp.logical_and(o >= 0, o < n),
                                     jnp.logical_and(s >= 2, jnp.logical_or(way == 0, s > 2))))
            def _():
                @pl.when(s > 2)
                def _():
                    across(0, o, other).wait_recv()
                halo_wait(0, o)
                block(0, o, a_buf, b_buf)

                @pl.when(jnp.logical_and(o == 0, has_up))
                def _():
                    halo(1, 0).start()

                @pl.when(jnp.logical_and(o == n - 1, has_down))
                def _():
                    halo(1, 1).start()
            return carry

        lax.fori_loop(0, 2, one, 0)
        return carry

    lax.fori_loop(1, n + 2, first, 0)

    def second(i, carry):
        o = jnp.where(i < n - 2, i + 1, jnp.where(i == n - 2, 0, n - 1))
        o = jnp.where(2 * me < n, o, n - 1 - o)

        @pl.when(o != me)
        def _():
            across(1, o, other).wait_recv()
        halo_wait(1, o)
        block(1, o, b_buf, None)

        if 0 in CHAINED:
            @pl.when(i > 0)
            def _():
                relay(0, i)
        return carry

    lax.fori_loop(0, n, second, 0)

    for d in range(1, depths):
        if d in CHAINED:
            for pos in range(1, n - 1):
                relay(d, pos)
    for d in range(depths):
        if d in CHAINED:
            out[d] = term[d, rows_of(me)]

            @pl.when(me > 0)
            def _():
                chain(d, me, 1).wait_recv()
                out[d] += cbuf[1, d, rows_of(me)]

            @pl.when(me < n - 1)
            def _():
                chain(d, me, 0).wait_recv()
                out[d] += cbuf[0, d, rows_of(me)]
        else:
            total = term[d, rows_of(me)]

            def add(k, total):
                o = lax.rem(me + k, n)
                summand(d, o, o).wait_recv()
                return total + rbuf[d, rows_of(o)]

            out[d] = lax.fori_loop(1, n, add, total)

    for d in range(depths):
        @pl.when(has_up)
        def _():
            halo(d, 0).wait_send()

        @pl.when(has_down)
        def _():
            halo(d, 1).wait_send()

        def drain(o, carry):
            if d not in DIRECT:
                @pl.when(jnp.logical_and(o <= me, me < n - 1))
                def _():
                    on_line(d, o, 1).wait_send()

                @pl.when(jnp.logical_and(o >= me, me > 0))
                def _():
                    on_line(d, o, 0).wait_send()

            @pl.when(o != me)
            def _():
                if d in DIRECT:
                    to_all(d, o).wait_send()
                across(d, o, shot).wait_send()
                chain(d, o, 1).wait_send()
            return carry

        lax.fori_loop(0, n, drain, 0)


def per_device(n, tiles, omega, wavefields, velocity, eta):
    depths, shard, cols = velocity.shape
    sides, parts, freqs, rows, _ = wavefields.shape
    padded = (sides, parts, freqs, rows + 2 * PAD, cols)
    dma = pltpu.SemaphoreType.DMA
    return pl.pallas_call(
        functools.partial(kernel, n, tiles),
        out_shape=jax.ShapeDtypeStruct((depths, shard, cols), jnp.float32),
        in_specs=[pl.BlockSpec(memory_space=pltpu.HBM)] * 4,
        out_specs=pl.BlockSpec(memory_space=pltpu.VMEM),
        scratch_shapes=[
            pltpu.VMEM(padded, jnp.float32),
            pltpu.VMEM(padded, jnp.float32),
            pltpu.VMEM((2, depths, rows, cols), jnp.float32),
            pltpu.VMEM((depths, rows, cols), jnp.float32),
            pltpu.VMEM((depths, rows, cols), jnp.float32),
            pltpu.VMEM((2, depths, rows, cols), jnp.float32),
            pltpu.VMEM((2 * cols, cols), jnp.bfloat16),
            pltpu.VMEM((shard, shard + 2 * PAD), jnp.bfloat16),
            pltpu.SMEM((freqs,), jnp.float32),
            dma((4,)),
            dma((2, depths, n)),
            dma((depths, n)),
            dma((depths, n)),
            dma((depths, n)),
            dma((depths, 2)),
            dma((depths, 2)),
            dma((depths, n)),
            dma((depths, n)),
            dma((2, depths, n)),
        ],
        compiler_params=pltpu.CompilerParams(
            collective_id=0, has_side_effects=True, vmem_limit_bytes=63 * 1024 * 1024),
    )(omega, wavefields, velocity, eta)


def solution(mesh):
    return jax.shard_map(
        functools.partial(per_device, mesh.shape["freq"], mesh.shape["tile"]),
        mesh=mesh,
        in_specs=(
            P("freq"),
            P("shot", None, "freq", "tile", None),
            P(None, ("tile", "freq"), None),
            P(None, ("tile", "freq"), None),
        ),
        out_specs=P("shot", ("tile", "freq"), None),
        check_vma=False,
    )
```

```python
import functools

import jax
import jax.numpy as jnp
from jax import lax
from jax.experimental import pallas as pl
from jax.experimental.pallas import tpu as pltpu
from jax.sharding import PartitionSpec as P

MESH = pl.DeviceIdType.MESH
CHAINED = ()
DIRECT = ()
EARLY = False
PAD = 16
HALO = 8

CENTRE = -980.0
WEIGHTS = ((1, 135.0), (2, -13.5), (3, 1.0))


def band(distance, centre):
    out = jnp.where(distance == 0, centre, 0.0)
    for shift, weight in WEIGHTS:
        out = jnp.where(jnp.abs(distance) == shift, weight, out)
    return out.astype(jnp.bfloat16)


def cos_sin(x):
    z = x * x
    c = -1.0 / 3628800.0
    for k in (1.0 / 40320.0, -1.0 / 720.0, 1.0 / 24.0, -0.5, 1.0):
        c = c * z + k
    s = 1.0 / 362880.0
    for k in (-1.0 / 5040.0, 1.0 / 120.0, -1.0 / 6.0, 1.0):
        s = s * z + k
    return c, s * x


def kernel(n, tiles, omega_hbm, wf, vel, eta, out, a_buf, b_buf, va, term, rbuf, cbuf,
           my_buf, mx_buf, omega_ref, local_sem, zs, zr, ys, yr, hs, hr, rs, rr, cr):
    depths = vel.shape[0]
    shard = vel.shape[1]
    rows, cols = wf.shape[3], wf.shape[4]
    freqs = wf.shape[2]
    me = lax.axis_index("freq")
    shot = lax.axis_index("shot")
    tile = lax.axis_index("tile")
    other = 1 - shot
    has_up = tile > 0
    has_down = tile < tiles - 1

    def rows_of(o):
        return pl.ds(pl.multiple_of(o * shard, shard), shard)

    load_v = pltpu.make_async_copy(vel, va.at[0, :, rows_of(me)], local_sem.at[0])
    load_e = pltpu.make_async_copy(eta, va.at[1, :, rows_of(me)], local_sem.at[1])
    load_f = pltpu.make_async_copy(wf, a_buf.at[:, :, :, pl.ds(PAD, rows)], local_sem.at[2])
    load_o = pltpu.make_async_copy(omega_hbm, omega_ref, local_sem.at[3])
    load_v.start()
    load_e.start()
    load_f.start()
    load_o.start()

    barrier = pltpu.get_barrier_semaphore()

    def greet(k, carry):
        @pl.when(k != me)
        def _():
            pl.semaphore_signal(barrier, inc=1, device_id={"freq": k}, device_id_type=MESH)
        return carry

    lax.fori_loop(0, n, greet, 0)
    pl.semaphore_signal(barrier, inc=1, device_id={"shot": other}, device_id_type=MESH)

    @pl.when(has_up)
    def _():
        pl.semaphore_signal(barrier, inc=1, device_id={"tile": tile - 1}, device_id_type=MESH)

    @pl.when(has_down)
    def _():
        pl.semaphore_signal(barrier, inc=1, device_id={"tile": tile + 1}, device_id_type=MESH)

    r = lax.broadcasted_iota(jnp.int32, (cols, cols), 0)
    c = lax.broadcasted_iota(jnp.int32, (cols, cols), 1)
    my = band(r - c, CENTRE)
    my_buf[0:cols] = my
    my_buf[cols:2 * cols] = my
    window = shard + 2 * PAD
    r = lax.broadcasted_iota(jnp.int32, (shard, window), 0)
    c = lax.broadcasted_iota(jnp.int32, (shard, window), 1)
    mx_buf[:, 0:window] = band(c - PAD - r, 0.0)
    for buf in (a_buf, b_buf):
        zeros = jnp.zeros(buf.shape[:3] + (PAD - HALO, cols), jnp.float32)
        buf[:, :, :, 0:PAD - HALO] = zeros
        buf[:, :, :, PAD + rows + HALO:2 * PAD + rows] = zeros

        @pl.when(jnp.logical_not(has_up))
        def _():
            buf[:, :, :, PAD - HALO:PAD] = jnp.zeros(buf.shape[:3] + (HALO, cols), jnp.float32)

        @pl.when(jnp.logical_not(has_down))
        def _():
            buf[:, :, :, PAD + rows:PAD + rows + HALO] = jnp.zeros(buf.shape[:3] + (HALO, cols), jnp.float32)

    pl.semaphore_wait(barrier, n + has_up.astype(jnp.int32) + has_down.astype(jnp.int32))

    def halo(d, slot):
        if d == 0:
            src = wf.at[:, :, :, pl.ds(0 if slot == 0 else rows - HALO, HALO)]
            buf = a_buf
        else:
            src = b_buf.at[:, :, :, pl.ds(PAD if slot == 0 else PAD + rows - HALO, HALO)]
            buf = b_buf
        dst = buf.at[:, :, :, pl.ds(PAD + rows if slot == 0 else PAD - HALO, HALO)]
        return pltpu.make_async_remote_copy(
            src_ref=src, dst_ref=dst, send_sem=hs.at[d, slot], recv_sem=hr.at[d, slot],
            device_id={"tile": tile - 1 if slot == 0 else tile + 1}, device_id_type=MESH)

    def on_line(d, o, way):
        slot = va.at[shot, d, rows_of(o)]
        return pltpu.make_async_remote_copy(
            src_ref=slot, dst_ref=slot, send_sem=zs.at[way, d, o], recv_sem=zr.at[d, o],
            device_id={"freq": me + 1 if way else me - 1}, device_id_type=MESH)

    def across(d, o, which):
        slot = va.at[which, d, rows_of(o)]
        return pltpu.make_async_remote_copy(
            src_ref=slot, dst_ref=slot, send_sem=ys.at[d, o], recv_sem=yr.at[d, o],
            device_id={"shot": other}, device_id_type=MESH)

    def summand(d, to, frm):
        return pltpu.make_async_remote_copy(
            src_ref=term.at[d, rows_of(to)], dst_ref=rbuf.at[d, rows_of(frm)],
            send_sem=rs.at[d, to], recv_sem=rr.at[d, frm],
            device_id={"freq": to}, device_id_type=MESH)

    def chain(d, o, way):
        return pltpu.make_async_remote_copy(
            src_ref=term.at[d, rows_of(o)], dst_ref=cbuf.at[way, d, rows_of(o)],
            send_sem=rs.at[d, o], recv_sem=cr.at[way, d, o],
            device_id={"freq": me + 1 if way else me - 1}, device_id_type=MESH)

    def relay(d, pos):
        def step(k, carry):
            for way, first in ((1, me == pos), (0, n - 1 - me == pos)):
                o = me + k if way else me - k

                @pl.when(jnp.logical_and(first, jnp.logical_and(o >= 0, o < n)))
                def _():
                    chain(d, o, way).wait_recv()
                    term[d, rows_of(o)] += cbuf[way, d, rows_of(o)]
                    chain(d, o, way).start()
            return carry

        lax.fori_loop(1, n, step, 0)

    def to_all(d, to):
        slot = va.at[shot, d, rows_of(me)]
        return pltpu.make_async_remote_copy(
            src_ref=slot, dst_ref=slot, send_sem=zs.at[0, d, to], recv_sem=zr.at[d, me],
            device_id={"freq": to}, device_id_type=MESH)

    def send_own(d):
        if d in DIRECT:
            def step(k, carry):
                for to in (me + k, me - k):
                    @pl.when(jnp.logical_and(to >= 0, to < n))
                    def _():
                        to_all(d, to).start()
                return carry

            lax.fori_loop(1, n, step, 0)
        else:
            @pl.when(me < n - 1)
            def _():
                on_line(d, me, 1).start()

            @pl.when(me > 0)
            def _():
                on_line(d, me, 0).start()

    def pass_on(d, dist):
        for way in (1, 0):
            o = me - dist if way else me + dist

            @pl.when(jnp.logical_and(o >= 0, o < n))
            def _():
                on_line(d, o, way).wait_recv()
                across(d, o, shot).start()
                if d not in DIRECT:
                    @pl.when(me < n - 1 if way else me > 0)
                    def _():
                        on_line(d, o, way).start()

    def block(d, o, src, dst):
        start = pl.multiple_of(o * shard, shard)
        v = va[0, d, pl.ds(start, shard)]
        e = va[1, d, pl.ds(start, shard)]
        inv = 1.0 / v
        lift = v * (1.0 + 2.0 * e) * (0.5 / 90.0)
        mx = mx_buf[:, 0:window]
        mx2 = jnp.concatenate([mx, mx], axis=1)
        total = None
        for w in range(freqs):
            om = jnp.full((1, cols), omega_ref[w], jnp.float32)
            theta = lift * (1.0 / om)
            cosine, sine = cos_sin(inv * (om * 0.01))
            mids, along, lhs = [], [], []
            for s in range(2):
                for k in range(2):
                    f = src[s, k, w, pl.ds(start, window)]
                    hi = f.astype(jnp.bfloat16)
                    lo = (f - hi.astype(jnp.float32)).astype(jnp.bfloat16)
                    mids.append(f[PAD:PAD + shard])
                    along.append(jnp.dot(mx2, jnp.concatenate([hi, lo], axis=0),
                                         preferred_element_type=jnp.float32))
                    lhs.append(jnp.concatenate([hi[PAD:PAD + shard], lo[PAD:PAD + shard]], axis=1))
            ydir = jnp.dot(jnp.concatenate(lhs, axis=0), my_buf[...], preferred_element_type=jnp.float32)
            laps = [along[i] + ydir[i * shard:(i + 1) * shard] for i in range(4)]
            outs = []
            for s in range(2):
                sign = -1.0 if s == 0 else 1.0
                re, im = mids[2 * s], mids[2 * s + 1]
                lre, lim = theta * laps[2 * s], theta * laps[2 * s + 1]
                if s == 0:
                    vre, vim = re + lim, im - lre
                    ore = cosine * vre + sine * vim
                    oim = cosine * vim - sine * vre
                else:
                    vre, vim = re - lim, im + lre
                    ore = cosine * vre - sine * vim
                    oim = cosine * vim + sine * vre
                outs.append((ore, oim))
                if dst is not None:
                    at = pl.ds(pl.multiple_of(start + PAD, 8), shard)
                    dst[s, 0, w, at] = ore
                    dst[s, 1, w, at] = oim
            part = outs[0][0] * outs[1][0] + outs[0][1] * outs[1][1]
            total = part if total is None else total + part
        term[d, pl.ds(start, shard)] = total

        if d in CHAINED:
            @pl.when(jnp.logical_and(o > me, me == 0))
            def _():
                chain(d, o, 1).start()

            @pl.when(jnp.logical_and(o < me, me == n - 1))
            def _():
                chain(d, o, 0).start()
        else:
            @pl.when(o != me)
            def _():
                summand(d, o, me).start()

    load_v.wait()
    load_e.wait()
    send_own(0)
    if EARLY:
        for d in range(1, depths):
            send_own(d)
    @pl.when(has_up)
    def _():
        halo(0, 0).start()

    @pl.when(has_down)
    def _():
        halo(0, 1).start()

    load_f.wait()
    load_o.wait()

    def halo_wait(d, o):
        @pl.when(jnp.logical_and(o == 0, has_up))
        def _():
            halo(d, 1).wait_recv()

        @pl.when(jnp.logical_and(o == n - 1, has_down))
        def _():
            halo(d, 0).wait_recv()

    def first(s, carry):
        @pl.when(s < n)
        def _():
            pass_on(0, s)

        if not EARLY:
            @pl.when(s == 1)
            def _():
                for d in range(1, depths):
                    send_own(d)

        @pl.when(jnp.logical_and(s > 1, s <= n))
        def _():
            for d in range(1, depths):
                pass_on(d, s - 1)

        def one(way, carry):
            o = jnp.where(way == 0, me - (s - 2), me + (s - 2))

            @pl.when(jnp.logical_and(jnp.logical_and(o >= 0, o < n),
                                     jnp.logical_and(s >= 2, jnp.logical_or(way == 0, s > 2))))
            def _():
                @pl.when(s > 2)
                def _():
                    across(0, o, other).wait_recv()
                halo_wait(0, o)
                block(0, o, a_buf, b_buf)

                @pl.when(jnp.logical_and(o == 0, has_up))
                def _():
                    halo(1, 0).start()

                @pl.when(jnp.logical_and(o == n - 1, has_down))
                def _():
                    halo(1, 1).start()
            return carry

        lax.fori_loop(0, 2, one, 0)
        return carry

    lax.fori_loop(1, n + 2, first, 0)

    def second(i, carry):
        o = jnp.where(i < n - 2, i + 1, jnp.where(i == n - 2, 0, n - 1))
        o = jnp.where(2 * me < n, o, n - 1 - o)

        @pl.when(o != me)
        def _():
            across(1, o, other).wait_recv()
        halo_wait(1, o)
        block(1, o, b_buf, None)

        if 0 in CHAINED:
            @pl.when(i > 0)
            def _():
                relay(0, i)
        return carry

    lax.fori_loop(0, n, second, 0)

    for d in range(1, depths):
        if d in CHAINED:
            for pos in range(1, n - 1):
                relay(d, pos)
    for d in range(depths):
        if d in CHAINED:
            out[d] = term[d, rows_of(me)]

            @pl.when(me > 0)
            def _():
                chain(d, me, 1).wait_recv()
                out[d] += cbuf[1, d, rows_of(me)]

            @pl.when(me < n - 1)
            def _():
                chain(d, me, 0).wait_recv()
                out[d] += cbuf[0, d, rows_of(me)]
        else:
            total = term[d, rows_of(me)]

            def add(k, total):
                o = lax.rem(me + k, n)
                summand(d, o, o).wait_recv()
                return total + rbuf[d, rows_of(o)]

            out[d] = lax.fori_loop(1, n, add, total)

    for d in range(depths):
        @pl.when(has_up)
        def _():
            halo(d, 0).wait_send()

        @pl.when(has_down)
        def _():
            halo(d, 1).wait_send()

        def drain(o, carry):
            if d not in DIRECT:
                @pl.when(jnp.logical_and(o <= me, me < n - 1))
                def _():
                    on_line(d, o, 1).wait_send()

                @pl.when(jnp.logical_and(o >= me, me > 0))
                def _():
                    on_line(d, o, 0).wait_send()

            @pl.when(o != me)
            def _():
                if d in DIRECT:
                    to_all(d, o).wait_send()
                across(d, o, shot).wait_send()
                chain(d, o, 1).wait_send()
            return carry

        lax.fori_loop(0, n, drain, 0)


def per_device(n, tiles, omega, wavefields, velocity, eta):
    depths, shard, cols = velocity.shape
    sides, parts, freqs, rows, _ = wavefields.shape
    padded = (sides, parts, freqs, rows + 2 * PAD, cols)
    dma = pltpu.SemaphoreType.DMA
    return pl.pallas_call(
        functools.partial(kernel, n, tiles),
        out_shape=jax.ShapeDtypeStruct((depths, shard, cols), jnp.float32),
        in_specs=[pl.BlockSpec(memory_space=pltpu.HBM)] * 4,
        out_specs=pl.BlockSpec(memory_space=pltpu.VMEM),
        scratch_shapes=[
            pltpu.VMEM(padded, jnp.float32),
            pltpu.VMEM(padded, jnp.float32),
            pltpu.VMEM((2, depths, rows, cols), jnp.float32),
            pltpu.VMEM((depths, rows, cols), jnp.float32),
            pltpu.VMEM((depths, rows, cols), jnp.float32),
            pltpu.VMEM((2, depths, rows, cols), jnp.float32),
            pltpu.VMEM((2 * cols, cols), jnp.bfloat16),
            pltpu.VMEM((shard, shard + 2 * PAD), jnp.bfloat16),
            pltpu.SMEM((freqs,), jnp.float32),
            dma((4,)),
            dma((2, depths, n)),
            dma((depths, n)),
            dma((depths, n)),
            dma((depths, n)),
            dma((depths, 2)),
            dma((depths, 2)),
            dma((depths, n)),
            dma((depths, n)),
            dma((2, depths, n)),
        ],
        compiler_params=pltpu.CompilerParams(
            collective_id=0, has_side_effects=True, vmem_limit_bytes=63 * 1024 * 1024),
    )(omega, wavefields, velocity, eta)


def solution(mesh):
    return jax.shard_map(
        functools.partial(per_device, mesh.shape["freq"], mesh.shape["tile"]),
        mesh=mesh,
        in_specs=(
            P("freq"),
            P("shot", None, "freq", "tile", None),
            P(None, ("tile", "freq"), None),
            P(None, ("tile", "freq"), None),
        ),
        out_specs=P("shot", ("tile", "freq"), None),
        check_vma=False,
    )
```
